512 devices in a mesh: dp: 8 (over x, core), expert: 64 (over z, y).
Axes of the slice: x: 4, y: 4, z: 16, core: 2. Of those that a mesh axis runs over, the one named last changes fastest.
Arguments:
- tokens: bfloat16 [16384, 4096], P('expert', 'dp'), may hold values from -6 to 6
- chosen: int32 [64, 64, 4], P('expert'), may hold values from 0 to 255, as said below
- counts: int32 [64, 64], P('expert'), may hold values from 0 to 4, as said below
- gates: float32 [64, 64, 4], P('expert'), may hold values from 0.25 to 1.5
- expert_gate: bfloat16 [64, 4096, 1024], P('expert', None, 'dp'), may hold values from -0.09375 to 0.09375
- expert_up: bfloat16 [64, 4096, 1024], P('expert', None, 'dp'), may hold values from -0.09375 to 0.09375
- expert_down: bfloat16 [64, 1024, 4096], P('expert', 'dp'), may hold values from -0.1875 to 0.1875
- shared_gate: bfloat16 [4096, 2048], P('expert', 'dp'), may hold values from -0.09375 to 0.09375
- shared_up: bfloat16 [4096, 2048], P('expert', 'dp'), may hold values from -0.09375 to 0.09375
- shared_down: bfloat16 [2048, 4096], P('dp', 'expert'), may hold values from -0.125 to 0.125
Outputs:
- mixed: bfloat16 [16384, 4096], P('expert', 'dp')
The draws below stay inside these ranges and needn't reach their ends.
Inputs may be any that keep to these rules, and one draw needn't show every extreme that they name: chosen[e, j, s] is a row among the 256 tokens of index j of expert; for each e and j the 4 rows are distinct; only the first counts[e, j] slots are live. `counts`: some expert has all 4 slots live for every index of expert.
All inputs are finite; a program needn't handle non-finite values.
Results may differ from the reference program's by a relative error of at most 0.019.
Values may be sent and summed in bfloat16 or wider, within the bound.
A program may use at most 64 MiB of HBM per device.

```python
import jax
import jax.numpy as jnp
from jax import lax

D = 4096
EH = 1024
SH = 2048
SHARED = 1
TOK_DEV = 256
SLOT = 4
EXPERTS = 64
TOKENS = 16384
N_DP = 8
N_EXPERT = 64


def draw_chosen(key, part):
    key = jax.random.fold_in(key, 11)
    subkeys = jax.random.split(key, EXPERTS * N_EXPERT)

    def first_rows(inner_key):
        return jax.random.permutation(inner_key, TOK_DEV)[:SLOT]
    picked = jax.vmap(first_rows)(subkeys)
    return picked.reshape(EXPERTS, N_EXPERT, SLOT).astype(jnp.int32)


def draw_counts(key, part):
    key = jax.random.fold_in(key, 23)
    count_key, full_key = jax.random.split(key)
    drawn = jax.random.randint(count_key, (EXPERTS, N_EXPERT), 0, SLOT + 1)
    fullest = jax.random.randint(full_key, (), 0, EXPERTS)
    expert_rank = jnp.arange(EXPERTS)[:, None]
    return jnp.where(expert_rank == fullest, SLOT, drawn).astype(jnp.int32)


def shard_levels(rng, shape, cuts, low, high):
    loudness = 1.0
    for dim, blocks in cuts:
        heights = jax.random.uniform(jax.random.fold_in(jax.random.fold_in(rng, 6), dim), (blocks,), jnp.float32, low / len(cuts), high / len(cuts))
        loudness = loudness * jnp.repeat(jnp.exp(heights), shape[dim] // blocks).reshape((-1,) + (1,) * (len(shape) - 1 - dim))
    return loudness


def gaussian(own_key, shape, scale, limit, shards=(), held_as=jnp.bfloat16):
    array = scale * jax.random.normal(own_key, shape, jnp.float32)
    if shards:
        array = array * shard_levels(own_key, shape, shards, -0.22, 0.18)
    return jnp.clip(array, -limit, limit).astype(held_as)


def setup_inputs(seed: int = 0) -> dict:
    arg_keys = jax.random.split(jax.random.key(seed), 11)
    tokens = gaussian(arg_keys[0], (TOKENS, D), 1.0, 6.0, ((0, 64), (1, 8)))
    chosen = draw_chosen(jax.random.fold_in(arg_keys[10], 71), 0)
    counts = draw_counts(jax.random.fold_in(arg_keys[10], 71), 0)
    gates = jnp.clip(0.25 + 1.25 * jax.random.uniform(arg_keys[3], (EXPERTS, N_EXPERT, SLOT), jnp.float32) ** shard_levels(arg_keys[3], (EXPERTS, N_EXPERT, SLOT), ((0, 64),), -0.2, 0.2), 0.25, 1.5)
    expert_gate = gaussian(arg_keys[4], (EXPERTS, D, EH), D ** -0.5, 0.09375, ((0, 64), (2, 8)))
    expert_up = gaussian(arg_keys[5], (EXPERTS, D, EH), D ** -0.5, 0.09375, ((0, 64), (2, 8)))
    expert_down = gaussian(arg_keys[6], (EXPERTS, EH, D), EH ** -0.5, 0.1875, ((0, 64), (1, 8)))
    shared_gate = gaussian(arg_keys[7], (D, SHARED * SH), D ** -0.5, 0.09375, ((0, 64), (1, 8)))
    shared_up = gaussian(arg_keys[8], (D, SHARED * SH), D ** -0.5, 0.09375, ((0, 64), (1, 8)))
    shared_down = gaussian(arg_keys[9], (SHARED * SH, D), (SHARED * SH) ** -0.5, 0.125, ((0, 8), (1, 64)))
    return {"tokens": tokens, "chosen": chosen, "counts": counts, "gates": gates, "expert_gate": expert_gate, "expert_up": expert_up, "expert_down": expert_down, "shared_gate": shared_gate, "shared_up": shared_up, "shared_down": shared_down}


def grouped_down(hidden, down):
    group_size = hidden.shape[1] // N_DP
    running = jnp.zeros((hidden.shape[0], down.shape[1]), jnp.float32)
    for group in range(N_DP):
        partial_sum = jnp.dot(hidden[:, group * group_size:(group + 1) * group_size], down[group * group_size:(group + 1) * group_size], preferred_element_type=jnp.float32)
        running = running + lax.optimization_barrier(partial_sum.astype(jnp.bfloat16)).astype(jnp.float32)
    return running


def reference(tokens, chosen, counts, gates, expert_gate, expert_up, expert_down, shared_gate, shared_up, shared_down):
    s_gate = jnp.dot(tokens, shared_gate, preferred_element_type=jnp.float32)
    s_up = jnp.dot(tokens, shared_up, preferred_element_type=jnp.float32)
    shared_hidden = (jax.nn.silu(s_gate) * s_up).astype(jnp.bfloat16)
    shared_out = grouped_down(shared_hidden, shared_down)
    owner_base = (jnp.arange(N_EXPERT, dtype=jnp.int32) * TOK_DEV)[None, :, None]
    token_index = (chosen + owner_base).astype(jnp.int32).reshape(EXPERTS, N_EXPERT * SLOT)
    live_mask = jnp.arange(SLOT, dtype=jnp.int32)[None, None, :] < counts[:, :, None]
    slot_weight = jnp.where(live_mask, gates, jnp.zeros_like(gates)).reshape(EXPERTS, N_EXPERT * SLOT)

    def one_expert(operands):
        index_row, w_gate, w_up, w_down, weight_row = operands
        picked = jnp.take(tokens, index_row, axis=0)
        e_gate = jnp.dot(picked, w_gate, preferred_element_type=jnp.float32)
        e_up = jnp.dot(picked, w_up, preferred_element_type=jnp.float32)
        e_hidden = (jax.nn.silu(e_gate) * e_up).astype(jnp.bfloat16)
        return (grouped_down(e_hidden, w_down) * weight_row[:, None]).astype(jnp.bfloat16)

    expert_out = lax.map(one_expert, (token_index, expert_gate, expert_up, expert_down, slot_weight))
    routed = jax.ops.segment_sum(expert_out.reshape(EXPERTS * N_EXPERT * SLOT, D).astype(jnp.float32), token_index.reshape(-1), num_segments=TOKENS)
    return (shared_out + routed).astype(jnp.bfloat16)
```

```python
import functools

import jax
import jax.numpy as jnp
from jax import lax
from jax.experimental import pallas as pl
from jax.experimental.pallas import tpu as pltpu
from jax.sharding import PartitionSpec as P

NC = 2
NY = 4
BF = jnp.bfloat16
F32 = jnp.float32
MESH = pl.DeviceIdType.MESH


def iota(shape, dim):
    return lax.broadcasted_iota(jnp.int32, shape, dim)


def dot(a, b):
    return jnp.dot(a, b, preferred_element_type=F32)


def dot_nt(a, b):
    return lax.dot_general(a, b, (((1,), (1,)), ((), ())), preferred_element_type=F32)


def dot_tn(a, b):
    return lax.dot_general(a, b, (((0,), (0,)), ((), ())), preferred_element_type=F32)


def silu_mul(g, u):
    return (g / (1.0 + jnp.exp(-g)) * u).astype(BF)


def kernel(
    ndp, nex, slots,
    tok, chz, gates, counts, eg, eu, ed, sg, su, sd,
    out,
    wt, tk, pk, c1, c2, onehot, pk0, pk1, pk2, w1, r1, w2, r2, shared_sum,
    et, eq, eun, ev, st, sq, sun, sv,
    ring_s, ring_r, set_s, set_r, x_s, x_r, rs_s, rs_r,
):
    NX = ndp // NC
    NZ = nex // NY
    T, F = tok.shape
    R = nex * slots
    RZ = NY * slots
    RY = NZ * slots
    d = lax.axis_index("dp")
    e = lax.axis_index("expert")
    x, c = d // NC, d % NC
    z, y = e // NY, e % NY
    mate = x * NC + (1 - c)
    WR = sg.shape[0]

    def zmod(v):
        return lax.rem(v + 2 * NZ, NZ)

    def at_z(k):
        return zmod(z + k) * NY + y

    def at_y(k):
        return z * NY + lax.rem(y + k, NY)

    def at_x(k):
        return lax.rem(x + k, NX) * NC + c

    def rc(src, dst, ss, rs, dp=None, ex=None):
        return pltpu.make_async_remote_copy(
            src_ref=src, dst_ref=dst, send_sem=ss, recv_sem=rs,
            device_id=(d if dp is None else dp, e if ex is None else ex), device_id_type=MESH,
        )

    def drain(view, sem):
        pltpu.make_async_copy(view, view, sem).wait()

    bar = pltpu.get_barrier_semaphore()

    def greet(dp, ex):
        pl.semaphore_signal(bar, inc=1, device_id=(dp, ex), device_id_type=MESH)

    def greet_z(k, carry):
        greet(d, at_z(k))
        return carry

    lax.fori_loop(1, NZ, greet_z, 0)
    for k in range(1, NY):
        greet(d, at_y(k))
    for k in range(1, NX):
        greet(at_x(k), e)
    greet(mate, e)

    def wrows(zc, n=1):
        return pl.ds(pl.multiple_of(zc * (NY * WR), NY * WR), NY * WR)

    def wrow1(zc, yc):
        return pl.ds(pl.multiple_of((zc * NY + yc) * WR, WR), WR)

    mine = wrow1(z, y)
    wt[0, mine, :] = sg[...]
    wt[1, mine, :] = su[...]
    wt[2, mine, :] = sd[...]
    tk[d] = tok[...]
    c1[z] = chz[z]
    pl.semaphore_wait(bar, (NZ - 1) + (NY - 1) + (NX - 1) + 1)

    def send_z(i, src, dst):
        def one(k, carry):
            zz = zmod(z + k)
            rc(src(zz), dst, set_s.at[i], set_r.at[i], ex=zz * NY + y).start()
            return carry
        lax.fori_loop(1, NZ, one, 0)

    def send_y(i, src, dst):
        for k in range(1, NY):
            yy = lax.rem(y + k, NY)
            rc(src(yy), dst, set_s.at[i], set_r.at[i], ex=z * NY + yy).start()

    CW = NZ // 2
    CCW = NZ - 1 - CW

    def bsend(k, side):
        rows = wrow1(zmod(z - k) if side == 0 else zmod(z + k), y)
        v = wt.at[pl.ds(0, 2), rows, :]
        return rc(v, v, ring_s.at[0, side, k], ring_r.at[0, side, k], ex=at_z(1 if side == 0 else -1))

    def asend(k, side):
        rows = wrows(zmod(z - k) if side == 0 else zmod(z + k))
        v = wt.at[2, rows, :]
        return rc(v, v, ring_s.at[1, side, k], ring_r.at[1, side, k], ex=at_z(1 if side == 0 else -1))

    def bspread(zc):
        v = wt.at[pl.ds(0, 2), wrow1(zc, y), :]
        send_y(0, lambda yy: v, v)

    def ring_b(k):
        if k == 0:
            bsend(0, 0).start()
            bsend(0, 1).start()
            bspread(z)
            return
        if k <= CW:
            bsend(k - 1, 0).wait_recv()
            if k < CW:
                bsend(k, 0).start()
        if k <= CCW:
            bsend(k - 1, 1).wait_recv()
            if k < CCW:
                bsend(k, 1).start()
        if k <= CW:
            bspread(zmod(z - k))
        if k <= CCW:
            bspread(zmod(z + k))

    def ring_a(k):
        if k == 0:
            asend(0, 0).start()
            asend(0, 1).start()
            return
        if k <= CW:
            asend(k - 1, 0).wait_recv()
            if k < CW:
                asend(k, 0).start()
        if k <= CCW:
            asend(k - 1, 1).wait_recv()
            if k < CCW:
                asend(k, 1).start()

    def dp_own(i, buf):
        for k in range(1, NX):
            rc(buf.at[d], buf.at[d], x_s.at[i, k], x_r.at[i, k], dp=at_x(k)).start()
        rc(buf.at[d], buf.at[d], x_s.at[i, 0], x_r.at[i, 0], dp=mate).start()

    def dp_pass(i, buf):
        order = sorted(range(1, NX), key=lambda k: min(k, NX - k))
        for k in order:
            src = buf.at[at_x(NX - k)]
            rc(src, src, x_s.at[i, k], x_r.at[i, k], dp=at_x(k)).wait_recv()
            rc(src, src, x_s.at[i, 0], x_r.at[i, 0], dp=mate).start()

    def dp_done(i, buf):
        drain(buf.at[pl.ds(0, NX)], x_r.at[i, 0])
        drain(buf.at[pl.ds(0, NX)], x_s.at[i, 0])
        for k in range(1, NX):
            drain(buf.at[0], x_s.at[i, k])

    def rs_start(i, block, tb, qb, ub):
        for n in range(NX):
            xx = lax.rem(x + 1 + n, NX)
            tb[n] = block(xx * NC + (1 - c)).astype(BF)
            rc(tb.at[n], qb.at[n], rs_s.at[i, n], rs_r.at[i, n], dp=mate).start()

    def rs_cross(i, block, tb, qb, ub, vb):
        own = None
        for n in range(NX):
            xx = lax.rem(x + 1 + n, NX)
            val = block(xx * NC + c).astype(BF).astype(F32)
            rc(tb.at[n], qb.at[n], rs_s.at[i, n], rs_r.at[i, n], dp=mate).wait_recv()
            val = val + qb[n].astype(F32)
            if n < NX - 1:
                ub[n] = val.astype(BF)
                rc(ub.at[n], vb.at[n], rs_s.at[i, NX], rs_r.at[i, NX], dp=xx * NC + c).start()
            else:
                own = val
        return own

    def rs_end(i, own, tb, ub, vb):
        drain(vb, rs_r.at[i, NX])
        total = own
        for n in range(NX - 1):
            total = total + vb[n].astype(F32)
        for n in range(NX):
            drain(tb.at[n], rs_s.at[i, n])
        drain(ub, rs_s.at[i, NX])
        return total

    def perm(src):
        r, q = iota((R, R), 0), iota((R, R), 1)
        want = ((r // slots) % NY) * RY + (r // RZ) * slots + r % slots
        return dot((want == q).astype(BF), src).astype(BF)

    def unperm(src):
        r, q = iota((R, R), 0), iota((R, R), 1)
        want = ((r // slots) % NZ) * RZ + (r // RY) * slots + r % slots
        return dot((want == q).astype(BF), src).astype(BF)

    send_z(1, lambda zz: chz.at[zz], c1.at[z])
    dp_own(0, tk)
    vd = wt.at[2, mine, :]
    send_y(2, lambda yy: vd, vd)
    ring_b(0)

    drain(c1.at[pl.ds(0, NZ - 1)], set_r.at[1])
    c2[y] = c1[...]
    send_y(3, lambda yy: c1, c2.at[y])

    drain(wt.at[2, pl.ds(0, (NY - 1) * WR), :], set_r.at[2])
    ring_a(0)
    ring_b(1)

    drain(c2.at[pl.ds(0, NY - 1)], set_r.at[3])
    ids = c2[...].reshape(nex, 128).astype(F32).astype(BF)
    rep = (iota((R, nex), 0) // slots == iota((R, nex), 1)).astype(BF)
    spread = dot(rep, ids)
    lane = y * slots + iota((R, 128), 0) % slots
    pick = jnp.sum(jnp.where(iota((R, 128), 1) == lane, spread, 0.0), axis=1, keepdims=True)
    onehot[...] = (pick.astype(jnp.int32) == iota((R, T), 1)).astype(BF)
    pk0[...] = dot(onehot[...], tok[...]).astype(BF).reshape(NY, RY, F)
    pk1[y] = pk0[y]
    send_y(4, lambda yy: pk0.at[yy], pk1.at[y])

    dp_pass(0, tk)
    ring_b(2)
    ring_a(1)

    drain(pk1.at[pl.ds(0, NY - 1)], set_r.at[4])
    pk2[...] = perm(pk1[...].reshape(R, F)).reshape(NZ, RZ, F)
    pk[d, z] = pk2[z]
    send_z(5, lambda zz: pk2.at[zz], pk.at[d, z])

    ring_b(3)
    ring_a(2)
    ring_b(4)

    drain(pk.at[d, pl.ds(0, NZ - 1)], set_r.at[5])
    dp_own(1, pk)
    ring_a(3)
    ring_b(5)
    dp_pass(1, pk)
    ring_a(4)
    ring_b(6)
    dp_done(1, pk)

    EH = eg.shape[-1]

    def e_step(n, carry):
        a = pk[n].reshape(R, F)
        return carry[0] + dot(a, eg[n]), carry[1] + dot(a, eu[n])

    zero = jnp.zeros((R, EH), F32)
    e_g, e_u = lax.fori_loop(0, ndp, e_step, (zero, zero))
    e_hidden = silu_mul(e_g, e_u)

    def e_block(n):
        return dot(e_hidden, ed[:, pl.ds(pl.multiple_of(n * F, F), F)])

    rs_start(0, e_block, et, eq, eun)
    ring_a(5)
    ring_b(7)
    e_own = rs_cross(0, e_block, et, eq, eun, ev)
    ring_b(8)
    ring_a(6)
    e_sum = rs_end(0, e_own, et, eun, ev)

    live = iota(gates.shape, 0) % slots < counts[...]
    weight = jnp.where(live, gates[...], 0.0)
    reps = R // gates.shape[0]
    tall = jnp.broadcast_to(weight[None], (reps,) + gates.shape).reshape(R, nex)
    column = jnp.sum(
        jnp.where(iota((R, nex), 0) // slots == iota((R, nex), 1), tall, 0.0), axis=1, keepdims=True
    )
    w1[...] = (e_sum * column).astype(BF).reshape(NZ, RZ, F)
    r1[z] = w1[z]
    send_z(6, lambda zz: w1.at[zz], r1.at[z])
    ring_a(7)

    drain(r1.at[pl.ds(0, NZ - 1)], set_r.at[6])
    w2[...] = unperm(r1[...].reshape(R, F)).reshape(NY, RY, F)
    r2[y] = w2[y]
    send_y(7, lambda yy: w2.at[yy], r2.at[y])
    ring_a(8)

    dp_done(0, tk)
    drain(wt.at[pl.ds(0, 2), pl.ds(0, NZ * (NY - 1) * WR), :], set_r.at[0])

    def s_step(n, carry):
        a = tk[n]
        rows = pl.ds(pl.multiple_of(n * F, F), F)
        return carry[0] + dot(a, wt[0, rows, :]), carry[1] + dot(a, wt[1, rows, :])

    zero = jnp.zeros((T, sg.shape[1]), F32)
    s_g, s_u = lax.fori_loop(0, ndp, s_step, (zero, zero))
    s_hidden = silu_mul(s_g, s_u)

    def s_block(n):
        return dot_nt(s_hidden, wt[2, pl.ds(pl.multiple_of(n * F, F), F), :])

    rs_start(1, s_block, st, sq, sun)
    s_own = rs_cross(1, s_block, st, sq, sun, sv)
    drain(r2.at[pl.ds(0, NY - 1)], set_r.at[7])
    routed = dot_tn(onehot[...], r2[...].reshape(R, F))
    shared_sum[...] = s_own + routed
    out[...] = rs_end(1, shared_sum[...], st, sun, sv).astype(BF)

    drain(wt.at[pl.ds(0, 2), pl.ds(0, NZ * (NY - 1) * WR), :], set_s.at[0])
    drain(c1.at[pl.ds(0, NZ - 1)], set_s.at[1])
    drain(wt.at[2, pl.ds(0, (NY - 1) * WR), :], set_s.at[2])
    drain(c2.at[pl.ds(0, NY - 1)], set_s.at[3])
    drain(pk1.at[pl.ds(0, NY - 1)], set_s.at[4])
    drain(pk2.at[pl.ds(0, NZ - 1)], set_s.at[5])
    drain(w1.at[pl.ds(0, NZ - 1)], set_s.at[6])
    drain(r2.at[pl.ds(0, NY - 1)], set_s.at[7])
    for k in range(CW):
        bsend(k, 0).wait_send()
        asend(k, 0).wait_send()
    for k in range(CCW):
        bsend(k, 1).wait_send()
        asend(k, 1).wait_send()


def shards(ndp, nex, tokens, chosen, counts, gates, eg, eu, ed, sg, su, sd):
    NX, NZ = ndp // NC, nex // NY
    slots = chosen.shape[2]
    T, F = tokens.shape
    D = F * ndp
    R = nex * slots
    RZ, RY = NY * slots, NZ * slots
    WR, SHD = sg.shape
    CW = NZ // 2
    chz = jnp.pad(chosen.reshape(NZ, 1, RZ), ((0, 0), (0, 0), (0, 128 - RZ)))
    gt = gates[0].T
    if slots < 8:
        gt = jnp.concatenate([gt] * (8 // slots), axis=0)
    vm = pl.BlockSpec(memory_space=pltpu.VMEM)
    return pl.pallas_call(
        functools.partial(kernel, ndp, nex, slots),
        out_shape=jax.ShapeDtypeStruct((T, F), BF),
        in_specs=[vm] * 10,
        out_specs=vm,
        scratch_shapes=[
            pltpu.VMEM((3, D, SHD), BF),
            pltpu.VMEM((ndp, T, F), BF),
            pltpu.VMEM((ndp, NZ, RZ, F), BF),
            pltpu.VMEM((NZ, 1, 128), jnp.int32),
            pltpu.VMEM((NY, NZ, 1, 128), jnp.int32),
            pltpu.VMEM((R, T), BF),
            pltpu.VMEM((NY, RY, F), BF),
            pltpu.VMEM((NY, RY, F), BF),
            pltpu.VMEM((NZ, RZ, F), BF),
            pltpu.VMEM((NZ, RZ, F), BF),
            pltpu.VMEM((NZ, RZ, F), BF),
            pltpu.VMEM((NY, RY, F), BF),
            pltpu.VMEM((NY, RY, F), BF),
            pltpu.VMEM((T, F), F32),
            pltpu.VMEM((NX, R, F), BF),
            pltpu.VMEM((NX, R, F), BF),
            pltpu.VMEM((NX - 1, R, F), BF),
            pltpu.VMEM((NX - 1, R, F), BF),
            pltpu.VMEM((NX, T, F), BF),
            pltpu.VMEM((NX, T, F), BF),
            pltpu.VMEM((NX - 1, T, F), BF),
            pltpu.VMEM((NX - 1, T, F), BF),
            pltpu.SemaphoreType.DMA((2, 2, CW)),
            pltpu.SemaphoreType.DMA((2, 2, CW)),
            pltpu.SemaphoreType.DMA((8,)),
            pltpu.SemaphoreType.DMA((8,)),
            pltpu.SemaphoreType.DMA((2, NX)),
            pltpu.SemaphoreType.DMA((2, NX)),
            pltpu.SemaphoreType.DMA((2, NX + 1)),
            pltpu.SemaphoreType.DMA((2, NX + 1)),
        ],
        compiler_params=pltpu.CompilerParams(
            collective_id=0, has_side_effects=True, vmem_limit_bytes=48 * 1024 * 1024
        ),
    )(
        tokens, chz, gt, counts,
        eg.reshape(ndp, F, eg.shape[-1]), eu.reshape(ndp, F, eu.shape[-1]), ed[0], sg, su, sd.T,
    )


def solution(mesh):
    return jax.shard_map(
        functools.partial(shards, mesh.shape["dp"], mesh.shape["expert"]),
        mesh=mesh,
        in_specs=(
            P("expert", "dp"),
            P("expert", None, None),
            P("expert", None),
            P("expert", None, None),
            P("expert", None, "dp"),
            P("expert", None, "dp"),
            P("expert", "dp", None),
            P("expert", "dp"),
            P("expert", "dp"),
            P("dp", "expert"),
        ),
        out_specs=P("expert", "dp"),
        check_vma=False,
    )
```

```python
import functools

import jax
import jax.numpy as jnp
from jax import lax
from jax.experimental import pallas as pl
from jax.experimental.pallas import tpu as pltpu
from jax.sharding import PartitionSpec as P

NC = 2
NY = 4
AH = 1
BF = jnp.bfloat16
F32 = jnp.float32
MESH = pl.DeviceIdType.MESH


def iota(shape, dim):
    return lax.broadcasted_iota(jnp.int32, shape, dim)


def div(v, n):
    return v >> (n.bit_length() - 1)


def mod(v, n):
    return v & (n - 1)


def dot(a, b):
    return jnp.dot(a, b, preferred_element_type=F32)


def dot_nt(a, b):
    return lax.dot_general(a, b, (((1,), (1,)), ((), ())), preferred_element_type=F32)


def dot_tn(a, b):
    return lax.dot_general(a, b, (((0,), (0,)), ((), ())), preferred_element_type=F32)


def silu_mul(g, u):
    return (g / (1.0 + jnp.exp(-g)) * u).astype(BF)


def kernel(
    ndp, nex, slots,
    tok, ch, gates, counts, eg, eu, ed, sg, su, sd,
    out,
    wt, tk, pk, egv, euv, edv, chz, c1, c2, onehot, pm, um, col,
    pk0, pk1, pk2, w1, r1, w2, r2, shared_sum,
    et, eq, eun, ev, st, sq, sun, sv,
    loc, ring_s, ring_r, set_s, set_r, x_s, x_r, rs_s, rs_r,
):
    NX = ndp // NC
    NZ = nex // NY
    T, F = tok.shape
    R = nex * slots
    RZ = NY * slots
    RY = NZ * slots
    HZ = NZ // 2
    RQ = R // 2
    OWN = NZ // 4 - 1
    d = lax.axis_index("dp")
    e = lax.axis_index("expert")
    x, c = div(d, NC), mod(d, NC)
    z, y = div(e, NY), mod(e, NY)
    mate = x * NC + (1 - c)
    WR = sg.shape[0]

    def zmod(v):
        return lax.rem(v + 2 * NZ, NZ)

    def at_z(k):
        return zmod(z + k) * NY + y

    def at_y(k):
        return z * NY + lax.rem(y + k, NY)

    def at_x(k):
        return lax.rem(x + k, NX) * NC + c

    def rc(src, dst, ss, rs, dp=None, ex=None):
        return pltpu.make_async_remote_copy(
            src_ref=src, dst_ref=dst, send_sem=ss, recv_sem=rs,
            device_id=(d if dp is None else dp, e if ex is None else ex), device_id_type=MESH,
        )

    def drain(view, sem):
        pltpu.make_async_copy(view, view, sem).wait()

    bar = pltpu.get_barrier_semaphore()

    def greet(dp, ex):
        pl.semaphore_signal(bar, inc=1, device_id=(dp, ex), device_id_type=MESH)

    def greet_z(k, carry):
        greet(d, at_z(k))
        return carry

    lax.fori_loop(1, NZ, greet_z, 0)
    for k in range(1, NY):
        greet(d, at_y(k))
    for k in range(1, NX):
        greet(at_x(k), e)
    greet(mate, e)

    def wrow1(zc, yc):
        return pl.ds(pl.multiple_of((zc * NY + yc) * WR, WR), WR)

    mine = wrow1(z, y)
    loads = [
        pltpu.make_async_copy(src, dst, loc.at[i])
        for i, (src, dst) in enumerate([
            (sg, wt.at[0, mine, :]), (su, wt.at[1, mine, :]), (sd, wt.at[2, mine, :]), (tok, tk.at[d]),
            (eg, egv), (eu, euv), (ed, edv),
        ])
    ]
    for load in loads:
        load.start()

    ids = jnp.zeros((NZ, 128), F32)
    for s in range(slots):
        row = ch[pl.ds(s, 1), :].astype(F32)
        own = jnp.where(div(iota((NZ, nex), 1), NY) == iota((NZ, nex), 0), row, 0.0).astype(BF)
        place = iota((nex, 128), 1) == mod(iota((nex, 128), 0), NY) * slots + s
        ids = ids + dot(own, place.astype(BF))
    chz[...] = ids.astype(jnp.int32).reshape(NZ, 1, 128)

    r, q = iota((R, R), 0), iota((R, R), 1)
    pm[...] = (mod(div(r, slots), NY) * RY + div(r, RZ) * slots + mod(r, slots) == q).astype(BF)
    zoff = mod(div(r, slots) - z + OWN + NZ, NZ)
    um[...] = (zoff * RZ + div(r, RY) * slots + mod(r, slots) == q).astype(BF)

    live = iota(gates.shape, 0) < counts[...]
    weight = jnp.where(live, gates[...], 0.0)
    for h in range(2):
        r, lane = iota((RQ, nex), 0), iota((RQ, nex), 1)
        owner = mod(z - (h * HZ - OWN) - div(r, RZ) + 2 * NZ, NZ) * NY + mod(div(r, slots), NY)
        picked = jnp.zeros((RQ, nex), F32)
        for s in range(slots):
            picked = jnp.where((lane == owner) & (mod(r, slots) == s), weight[s:s + 1, :], picked)
        col[h] = jnp.sum(picked, axis=1, keepdims=True)

    for load in loads[:4]:
        load.wait()
    pl.semaphore_wait(bar, (NZ - 1) + (NY - 1) + (NX - 1) + 1)

    def send_z(i, src, dst):
        def one(k, carry):
            zz = zmod(z + k)
            rc(src(zz), dst, set_s.at[i], set_r.at[i], ex=zz * NY + y).start()
            return carry
        lax.fori_loop(1, NZ, one, 0)

    def send_slots(i, h, sign, src, dst):
        def one(s, carry):
            zz = zmod(z + sign * (s - OWN))
            rc(src(zz, s - h * HZ), dst(s), set_s.at[i], set_r.at[i], ex=zz * NY + y).start()
            return carry
        if h == 0:
            lax.fori_loop(0, OWN, one, 0)
            lax.fori_loop(OWN + 1, HZ, one, 0)
        else:
            lax.fori_loop(HZ, NZ, one, 0)

    def send_y(i, src, dst):
        for k in range(1, NY):
            yy = lax.rem(y + k, NY)
            rc(src(yy), dst, set_s.at[i], set_r.at[i], ex=z * NY + yy).start()

    CW = NZ // 2
    CCW = NZ - 1 - CW

    def bsend(k, side):
        rows = wrow1(zmod(z - k) if side == 0 else zmod(z + k), y)
        v = wt.at[pl.ds(0, 2), rows, :]
        return rc(v, v, ring_s.at[0, side, k], ring_r.at[0, side, k], ex=at_z(1 if side == 0 else -1))

    def asend(k, side, h):
        zc = zmod(z - k) if side == 0 else zmod(z + k)
        n = NY * WR // AH
        v = wt.at[2, pl.ds(pl.multiple_of(zc * (NY * WR) + h * n, n), n), :]
        return rc(v, v, ring_s.at[1 + h, side, k], ring_r.at[1 + h, side, k], ex=at_z(1 if side == 0 else -1))

    def bspread(zc):
        v = wt.at[pl.ds(0, 2), wrow1(zc, y), :]
        send_y(0, lambda yy: v, v)

    def ring_b(k):
        if k == 0:
            bsend(0, 0).start()
            bsend(0, 1).start()
            bspread(z)
            return
        if k <= CW:
            bsend(k - 1, 0).wait_recv()
            if k < CW:
                bsend(k, 0).start()
        if k <= CCW:
            bsend(k - 1, 1).wait_recv()
            if k < CCW:
                bsend(k, 1).start()
        if k <= CW:
            bspread(zmod(z - k))
        if k <= CCW:
            bspread(zmod(z + k))

    def ring_a(k):
        for h in range(AH):
            if k == 0:
                asend(0, 0, h).start()
                asend(0, 1, h).start()
                continue
            if k <= CW:
                asend(k - 1, 0, h).wait_recv()
                if k < CW:
                    asend(k, 0, h).start()
            if k <= CCW:
                asend(k - 1, 1, h).wait_recv()
                if k < CCW:
                    asend(k, 1, h).start()

    def ring(k):
        if k <= CW:
            ring_b(k)
        if 1 <= k <= CW + 1:
            ring_a(k - 1)

    XORDER = sorted(range(1, NX), key=lambda k: min(k, NX - k))

    def dp_own(i, buf):
        for k in range(1, NX):
            rc(buf(d), buf(d), x_s.at[i, k], x_r.at[i, k], dp=at_x(k)).start()
        rc(buf(d), buf(d), x_s.at[i, 0], x_r.at[i, 0], dp=mate).start()

    def dp_pass(i, buf):
        for k in XORDER:
            src = buf(at_x(NX - k))
            rc(src, src, x_s.at[i, k], x_r.at[i, k], dp=at_x(k)).wait_recv()
            rc(src, src, x_s.at[i, 0], x_r.at[i, 0], dp=mate).start()

    def dp_done(i, buf):
        drain(buf(pl.ds(0, NX)), x_r.at[i, 0])

    def dp_sent(i, buf):
        drain(buf(pl.ds(0, NX)), x_s.at[i, 0])
        for k in range(1, NX):
            drain(buf(0), x_s.at[i, k])

    def rs_start(i, block, tb, qb):
        for n in range(NX):
            xx = lax.rem(x + 1 + n, NX)
            tb[n] = block(xx * NC + (1 - c)).astype(BF)
            rc(tb.at[n], qb.at[n], rs_s.at[i, n], rs_r.at[i, n], dp=mate).start()

    def rs_cross(i, block, tb, qb, ub, vb):
        for n in range(NX):
            xx = lax.rem(x + 1 + n, NX)
            val = block(xx * NC + c).astype(BF).astype(F32)
            rc(tb.at[n], qb.at[n], rs_s.at[i, n], rs_r.at[i, n], dp=mate).wait_recv()
            ub[n] = (val + qb[n].astype(F32)).astype(BF)
            if n < NX - 1:
                rc(ub.at[n], vb.at[n], rs_s.at[i, NX], rs_r.at[i, NX], dp=xx * NC + c).start()

    def rs_end(i, ub, vb):
        drain(vb, rs_r.at[i, NX])
        total = ub[NX - 1].astype(F32)
        for n in range(NX - 1):
            total = total + vb[n].astype(F32)
        return total

    def rs_sent(i, tb, vb):
        for n in range(NX):
            drain(tb.at[n], rs_s.at[i, n])
        drain(vb, rs_s.at[i, NX])

    def tkb(n):
        return tk.at[n]

    def pkb(h):
        return lambda n: pk.at[h, n]

    EH = eg.shape[-1]
    hidden = [None, None, None]

    def e_up(h):
        def step(n, carry):
            a = pk[h, n].reshape(RQ, F)
            return carry[0] + dot(a, egv[n]), carry[1] + dot(a, euv[n])
        zero = jnp.zeros((RQ, EH), F32)
        g, u = lax.fori_loop(0, ndp, step, (zero, zero))
        hidden[h] = silu_mul(g, u)

    def e_block(h):
        return lambda n: dot(hidden[h], edv[:, pl.ds(pl.multiple_of(n * F, F), F)])

    def e_start(h):
        e_up(h)
        rs_start(h, e_block(h), et.at[h], eq.at[h])

    def e_cross(h):
        rs_cross(h, e_block(h), et.at[h], eq.at[h], eun.at[h], ev.at[h])

    def e_end(h):
        w1[h] = (rs_end(h, eun.at[h], ev.at[h]) * col[h]).astype(BF).reshape(HZ, RZ, F)
        if h == 0:
            r1[OWN] = w1[0, OWN]
        send_slots(8 + h, h, -1, lambda zz, s: w1.at[h, s], lambda s: r1.at[s])

    def z_in(h):
        n = HZ - 1 if h == 0 else HZ
        drain(pk.at[h, d, pl.ds(0, n)], set_r.at[5 + h])
        dp_own(1 + h, pkb(h))

    send_z(1, lambda zz: chz.at[zz], c1.at[z])
    vd = wt.at[2, mine, :]
    send_y(2, lambda yy: vd, vd)
    c1[z] = chz[z]
    ring_b(0)
    dp_own(0, tkb)
    drain(wt.at[2, pl.ds(0, (NY - 1) * WR), :], set_r.at[2])
    ring(1)

    drain(c1.at[pl.ds(0, NZ - 1)], set_r.at[1])
    send_y(3, lambda yy: c1, c2.at[y])
    c2[y] = c1[...]
    dp_pass(0, tkb)
    ring(2)

    drain(c2.at[pl.ds(0, NY - 1)], set_r.at[3])
    ids = c2[...].reshape(nex, 128).astype(F32).astype(BF)
    rep = (div(iota((R, nex), 0), slots) == iota((R, nex), 1)).astype(BF)
    spread = dot(rep, ids)
    lane = y * slots + mod(iota((R, 128), 0), slots)
    pick = jnp.sum(jnp.where(iota((R, 128), 1) == lane, spread, 0.0), axis=1, keepdims=True)
    onehot[...] = (pick.astype(jnp.int32) == iota((R, T), 1)).astype(BF)
    pk0[...] = dot(onehot[...], tk[d]).astype(BF).reshape(NY, RY, F)
    send_y(4, lambda yy: pk0.at[yy], pk1.at[y])
    pk1[y] = pk0[y]
    ring(3)

    drain(pk1.at[pl.ds(0, NY - 1)], set_r.at[4])
    pk2[...] = dot(pm[...], pk1[...].reshape(R, F)).astype(BF).reshape(NZ, RZ, F)
    send_slots(5, 0, 1, lambda zz, s: pk2.at[zz], lambda s: pk.at[0, d, s])
    send_slots(6, 1, 1, lambda zz, s: pk2.at[zz], lambda s: pk.at[1, d, s - HZ])
    pk[0, d, OWN] = pk2[z]
    ring(4)

    z_in(0)
    ring(5)
    z_in(1)
    ring(6)
    dp_pass(1, pkb(0))
    for load in loads[4:]:
        load.wait()
    dp_done(1, pkb(0))
    e_start(0)
    e_cross(0)
    ring(7)
    dp_pass(2, pkb(1))
    dp_done(2, pkb(1))
    e_start(1)
    e_cross(1)
    e_end(0)
    ring(8)
    ring(9)

    dp_done(0, tkb)
    drain(wt.at[pl.ds(0, 2), pl.ds(0, NZ * (NY - 1) * WR), :], set_r.at[0])

    def s_step(n, carry):
        a = tk[n]
        rows = pl.ds(pl.multiple_of(n * F, F), F)
        return carry[0] + dot(a, wt[0, rows, :]), carry[1] + dot(a, wt[1, rows, :])

    def s_block(n):
        return dot_nt(s_hidden, wt[2, pl.ds(pl.multiple_of(n * F, F), F), :])

    zero = jnp.zeros((T, sg.shape[1]), F32)
    s_g, s_u = lax.fori_loop(0, ndp, s_step, (zero, zero))
    s_hidden = silu_mul(s_g, s_u)
    rs_start(3, s_block, st, sq)
    e_end(1)
    rs_cross(3, s_block, st, sq, sun, sv)

    drain(r1.at[pl.ds(0, HZ - 1)], set_r.at[8])
    drain(r1.at[pl.ds(0, HZ)], set_r.at[9])
    w2[...] = dot(um[...], r1[...].reshape(R, F)).astype(BF).reshape(NY, RY, F)
    send_y(7, lambda yy: w2.at[yy], r2.at[y])
    r2[y] = w2[y]
    shared_sum[...] = rs_end(3, sun, sv)
    drain(r2.at[pl.ds(0, NY - 1)], set_r.at[7])
    out[...] = (shared_sum[...] + dot_tn(onehot[...], r2[...].reshape(R, F))).astype(BF)

    drain(wt.at[pl.ds(0, 2), pl.ds(0, NZ * (NY - 1) * WR), :], set_s.at[0])
    drain(c1.at[pl.ds(0, NZ - 1)], set_s.at[1])
    drain(wt.at[2, pl.ds(0, (NY - 1) * WR), :], set_s.at[2])
    drain(c2.at[pl.ds(0, NY - 1)], set_s.at[3])
    drain(pk1.at[pl.ds(0, NY - 1)], set_s.at[4])
    drain(pk2.at[pl.ds(0, HZ - 1)], set_s.at[5])
    drain(pk2.at[pl.ds(0, HZ)], set_s.at[6])
    drain(r2.at[pl.ds(0, NY - 1)], set_s.at[7])
    drain(r1.at[pl.ds(0, HZ - 1)], set_s.at[8])
    drain(r1.at[pl.ds(0, HZ)], set_s.at[9])
    dp_sent(0, tkb)
    for h in range(2):
        dp_sent(1 + h, pkb(h))
        rs_sent(h, et.at[h], ev.at[h])
    rs_sent(3, st, sv)
    for side, n in ((0, CW), (1, CCW)):
        for k in range(n):
            bsend(k, side).wait_send()
            for h in range(AH):
                asend(k, side, h).wait_send()


def shards(ndp, nex, tokens, chosen, counts, gates, eg, eu, ed, sg, su, sd):
    NX, NZ = ndp // NC, nex // NY
    slots = chosen.shape[2]
    T, F = tokens.shape
    D = F * ndp
    R = nex * slots
    RZ, RY = NY * slots, NZ * slots
    HZ, RQ = NZ // 2, R // 2
    WR, SHD = sg.shape
    EHD = eg.shape[-1]
    CW = NZ // 2
    vm = pl.BlockSpec(memory_space=pltpu.VMEM)
    hbm = pl.BlockSpec(memory_space=pltpu.HBM)
    return pl.pallas_call(
        functools.partial(kernel, ndp, nex, slots),
        out_shape=jax.ShapeDtypeStruct((T, F), BF),
        in_specs=[hbm, vm, vm, vm] + [hbm] * 6,
        out_specs=vm,
        scratch_shapes=[
            pltpu.VMEM((3, D, SHD), BF),
            pltpu.VMEM((ndp, T, F), BF),
            pltpu.VMEM((2, ndp, HZ, RZ, F), BF),
            pltpu.VMEM((ndp, F, EHD), BF),
            pltpu.VMEM((ndp, F, EHD), BF),
            pltpu.VMEM((EHD, D), BF),
            pltpu.VMEM((NZ, 1, 128), jnp.int32),
            pltpu.VMEM((NZ, 1, 128), jnp.int32),
            pltpu.VMEM((NY, NZ, 1, 128), jnp.int32),
            pltpu.VMEM((R, T), BF),
            pltpu.VMEM((R, R), BF),
            pltpu.VMEM((R, R), BF),
            pltpu.VMEM((2, RQ, 1), F32),
            pltpu.VMEM((NY, RY, F), BF),
            pltpu.VMEM((NY, RY, F), BF),
            pltpu.VMEM((NZ, RZ, F), BF),
            pltpu.VMEM((2, HZ, RZ, F), BF),
            pltpu.VMEM((NZ, RZ, F), BF),
            pltpu.VMEM((NY, RY, F), BF),
            pltpu.VMEM((NY, RY, F), BF),
            pltpu.VMEM((T, F), F32),
            pltpu.VMEM((2, NX, RQ, F), BF),
            pltpu.VMEM((2, NX, RQ, F), BF),
            pltpu.VMEM((2, NX, RQ, F), BF),
            pltpu.VMEM((2, NX - 1, RQ, F), BF),
            pltpu.VMEM((NX, T, F), BF),
            pltpu.VMEM((NX, T, F), BF),
            pltpu.VMEM((NX, T, F), BF),
            pltpu.VMEM((NX - 1, T, F), BF),
            pltpu.SemaphoreType.DMA((7,)),
            pltpu.SemaphoreType.DMA((1 + AH, 2, CW)),
            pltpu.SemaphoreType.DMA((1 + AH, 2, CW)),
            pltpu.SemaphoreType.DMA((10,)),
            pltpu.SemaphoreType.DMA((10,)),
            pltpu.SemaphoreType.DMA((3, NX)),
            pltpu.SemaphoreType.DMA((3, NX)),
            pltpu.SemaphoreType.DMA((4, NX + 1)),
            pltpu.SemaphoreType.DMA((4, NX + 1)),
        ],
        compiler_params=pltpu.CompilerParams(
            collective_id=0, has_side_effects=True, vmem_limit_bytes=60 * 1024 * 1024
        ),
    )(
        tokens, chosen[0].T, gates[0].T, counts,
        eg.reshape(ndp, F, EHD), eu.reshape(ndp, F, EHD), ed[0], sg, su, sd.T,
    )


def solution(mesh):
    return jax.shard_map(
        functools.partial(shards, mesh.shape["dp"], mesh.shape["expert"]),
        mesh=mesh,
        in_specs=(
            P("expert", "dp"),
            P("expert", None, None),
            P("expert", None),
            P("expert", None, None),
            P("expert", None, "dp"),
            P("expert", None, "dp"),
            P("expert", "dp", None),
            P("expert", "dp"),
            P("expert", "dp"),
            P("dp", "expert"),
        ),
        out_specs=P("expert", "dp"),
        check_vma=False,
    )
```

```python
import functools

import jax
import jax.numpy as jnp
from jax import lax
from jax.experimental import pallas as pl
from jax.experimental.pallas import tpu as pltpu
from jax.sharding import PartitionSpec as P

NC = 2
NY = 4

STEPS = (
    ("start", "dy", "r1", "iz", "r2", "iy", "r3", "oy", "r4", "tk", "z0", "r5", "z1", "r6"),
    ("g0", "e0", "x0", "r7", "g1", "e1", "x1", "r8", "w0", "r9"),
    ("su", "w1", "ss", "sx", "bz", "se", "by"),
)


def ORDER(last):
    names = [name for part in STEPS for name in part]
    return [n for n in names if not (n[0] == "r" and int(n[1:]) > last)]


AH = 1
BF = jnp.bfloat16
F32 = jnp.float32
MESH = pl.DeviceIdType.MESH


def iota(shape, dim):
    return lax.broadcasted_iota(jnp.int32, shape, dim)


def div(v, n):
    return v >> (n.bit_length() - 1)


def mod(v, n):
    return v & (n - 1)


def dot(a, b):
    return jnp.dot(a, b, preferred_element_type=F32)


def dot_nt(a, b):
    return lax.dot_general(a, b, (((1,), (1,)), ((), ())), preferred_element_type=F32)


def dot_tn(a, b):
    return lax.dot_general(a, b, (((0,), (0,)), ((), ())), preferred_element_type=F32)


def silu_mul(g, u):
    return (g / (1.0 + jnp.exp(-g)) * u).astype(BF)


def kernel(
    ndp, nex, slots,
    tok, ch, gates, counts, eg, eu, ed, sg, su, sd,
    out,
    wt, tk, pk, egv, euv, edv, chz, c1, c2, onehot, pm, um, col,
    pk0, pk1, pk2, w1, r1, w2, r2, shared_sum,
    et, eq, eun, ev, st, sq, sun, sv,
    loc, sp_r, ring_s, ring_r, set_s, set_r, x_s, x_r, rs_s, rs_r,
):
    NX = ndp // NC
    NZ = nex // NY
    T, F = tok.shape
    R = nex * slots
    RZ = NY * slots
    RY = NZ * slots
    HZ = NZ // 2
    RQ = R // 2
    OWN = NZ // 4 - 1
    d = lax.axis_index("dp")
    e = lax.axis_index("expert")
    x, c = div(d, NC), mod(d, NC)
    z, y = div(e, NY), mod(e, NY)
    mate = x * NC + (1 - c)
    WR = sg.shape[0]

    def zmod(v):
        return lax.rem(v + 2 * NZ, NZ)

    def at_z(k):
        return zmod(z + k) * NY + y

    def at_y(k):
        return z * NY + lax.rem(y + k, NY)

    def at_x(k):
        return lax.rem(x + k, NX) * NC + c

    def rc(src, dst, ss, rs, dp=None, ex=None):
        return pltpu.make_async_remote_copy(
            src_ref=src, dst_ref=dst, send_sem=ss, recv_sem=rs,
            device_id=(d if dp is None else dp, e if ex is None else ex), device_id_type=MESH,
        )

    def drain(view, sem):
        pltpu.make_async_copy(view, view, sem).wait()

    bar = pltpu.get_barrier_semaphore()

    def greet(dp, ex):
        pl.semaphore_signal(bar, inc=1, device_id=(dp, ex), device_id_type=MESH)

    def greet_z(k, carry):
        greet(d, at_z(k))
        return carry

    lax.fori_loop(1, NZ, greet_z, 0)
    for k in range(1, NY):
        greet(d, at_y(k))
    for k in range(1, NX):
        greet(at_x(k), e)
    greet(mate, e)

    def wrow1(zc, yc):
        return pl.ds(pl.multiple_of((zc * NY + yc) * WR, WR), WR)

    mine = wrow1(z, y)
    loads = [
        pltpu.make_async_copy(src, dst, loc.at[i])
        for i, (src, dst) in enumerate([
            (sg, wt.at[0, mine, :]), (su, wt.at[1, mine, :]), (sd, wt.at[2, mine, :]), (tok, tk.at[d]),
            (eg, egv), (eu, euv), (ed, edv),
        ])
    ]
    for load in loads:
        load.start()

    ids = jnp.zeros((NZ, 128), F32)
    for s in range(slots):
        row = ch[pl.ds(s, 1), :].astype(F32)
        own = jnp.where(div(iota((NZ, nex), 1), NY) == iota((NZ, nex), 0), row, 0.0).astype(BF)
        place = iota((nex, 128), 1) == mod(iota((nex, 128), 0), NY) * slots + s
        ids = ids + dot(own, place.astype(BF))
    chz[...] = ids.astype(jnp.int32).reshape(NZ, 1, 128)

    r, q = iota((R, R), 0), iota((R, R), 1)
    pm[...] = (mod(div(r, slots), NY) * RY + div(r, RZ) * slots + mod(r, slots) == q).astype(BF)
    zoff = mod(div(r, slots) - z + OWN + NZ, NZ)
    um[...] = (zoff * RZ + div(r, RY) * slots + mod(r, slots) == q).astype(BF)

    live = iota(gates.shape, 0) < counts[...]
    weight = jnp.where(live, gates[...], 0.0)
    for h in range(2):
        r, lane = iota((RQ, nex), 0), iota((RQ, nex), 1)
        owner = mod(z - (h * HZ - OWN) - div(r, RZ) + 2 * NZ, NZ) * NY + mod(div(r, slots), NY)
        picked = jnp.zeros((RQ, nex), F32)
        for s in range(slots):
            picked = jnp.where((lane == owner) & (mod(r, slots) == s), weight[s:s + 1, :], picked)
        col[h] = jnp.sum(picked, axis=1, keepdims=True)

    for load in loads[:4]:
        load.wait()
    pl.semaphore_wait(bar, (NZ - 1) + (NY - 1) + (NX - 1) + 1)

    def send_z(i, src, dst):
        def one(k, carry):
            zz = zmod(z + k)
            rc(src(zz), dst, set_s.at[i], set_r.at[i], ex=zz * NY + y).start()
            return carry
        lax.fori_loop(1, NZ, one, 0)

    def send_slots(i, h, sign, src, dst):
        def one(s, carry):
            zz = zmod(z + sign * (s - OWN))
            rc(src(zz, s - h * HZ), dst(s), set_s.at[i], set_r.at[i], ex=zz * NY + y).start()
            return carry
        if h == 0:
            lax.fori_loop(0, OWN, one, 0)
            lax.fori_loop(OWN + 1, HZ, one, 0)
        else:
            lax.fori_loop(HZ, NZ, one, 0)

    def send_y(i, src, dst):
        for k in range(1, NY):
            yy = lax.rem(y + k, NY)
            rc(src(yy), dst, set_s.at[i], set_r.at[i], ex=z * NY + yy).start()

    CW = NZ // 2
    CCW = NZ - 1 - CW

    def bsend(k, side):
        rows = wrow1(zmod(z - k) if side == 0 else zmod(z + k), y)
        v = wt.at[pl.ds(0, 2), rows, :]
        return rc(v, v, ring_s.at[0, side, k], ring_r.at[0, side, k], ex=at_z(1 if side == 0 else -1))

    def asend(k, side, h):
        zc = zmod(z - k) if side == 0 else zmod(z + k)
        n = NY * WR // AH
        v = wt.at[2, pl.ds(pl.multiple_of(zc * (NY * WR) + h * n, n), n), :]
        return rc(v, v, ring_s.at[1 + h, side, k], ring_r.at[1 + h, side, k], ex=at_z(1 if side == 0 else -1))

    def spread_to(j, zc, yc, side):
        v = wt.at[pl.ds(0, 2), wrow1(zc, yc), :]
        return rc(v, v, set_s.at[0], sp_r.at[side, j], ex=at_y(1 if side == 0 else NY - 1))

    def bspread(j, zc):
        spread_to(j, zc, y, 0).start()
        spread_to(j, zc, y, 1).start()

    def bpass(j, zc):
        for side in range(2):
            yc = lax.rem(y + (NY - 1 if side == 0 else 1), NY)
            spread_to(j, zc, yc, side).wait_recv()
            v = wt.at[side, wrow1(zc, yc), :]
            rc(v, v, set_s.at[0], set_r.at[0], ex=at_y(1 if side == 0 else NY - 1)).start()

    def bround(k, do):
        if k == 0:
            do(0, z)
        if 1 <= k <= CW:
            do(2 * k - 1, zmod(z - k))
        if 1 <= k <= CCW:
            do(2 * k, zmod(z + k))

    def ring_b(k):
        if k == 0:
            bsend(0, 0).start()
            bsend(0, 1).start()
            bround(0, bspread)
            return
        if k <= CW:
            bsend(k - 1, 0).wait_recv()
            if k < CW:
                bsend(k, 0).start()
        if k <= CCW:
            bsend(k - 1, 1).wait_recv()
            if k < CCW:
                bsend(k, 1).start()
        bround(k, bspread)

    def ring_a(k):
        for h in range(AH):
            if k == 0:
                asend(0, 0, h).start()
                asend(0, 1, h).start()
                continue
            if k <= CW:
                asend(k - 1, 0, h).wait_recv()
                if k < CW:
                    asend(k, 0, h).start()
            if k <= CCW:
                asend(k - 1, 1, h).wait_recv()
                if k < CCW:
                    asend(k, 1, h).start()

    def ring(k):
        if k <= CW:
            ring_b(k)
        bround(k - 1, bpass)
        if 1 <= k <= CW + 1:
            ring_a(k - 1)

    XORDER = sorted(range(1, NX), key=lambda k: min(k, NX - k))

    def dp_own(i, buf):
        for k in range(1, NX):
            rc(buf(d), buf(d), x_s.at[i, k], x_r.at[i, k], dp=at_x(k)).start()
        rc(buf(d), buf(d), x_s.at[i, 0], x_r.at[i, 0], dp=mate).start()

    def dp_pass(i, buf):
        for k in XORDER:
            src = buf(at_x(NX - k))
            rc(src, src, x_s.at[i, k], x_r.at[i, k], dp=at_x(k)).wait_recv()
            rc(src, src, x_s.at[i, 0], x_r.at[i, 0], dp=mate).start()

    def dp_done(i, buf):
        drain(buf(pl.ds(0, NX)), x_r.at[i, 0])

    def dp_sent(i, buf):
        drain(buf(pl.ds(0, NX)), x_s.at[i, 0])
        for k in range(1, NX):
            drain(buf(0), x_s.at[i, k])

    def rs_start(i, block, tb, qb):
        for n in range(NX):
            xx = lax.rem(x + 1 + n, NX)
            tb[n] = block(xx * NC + (1 - c)).astype(BF)
            rc(tb.at[n], qb.at[n], rs_s.at[i, n], rs_r.at[i, n], dp=mate).start()

    def rs_cross(i, block, tb, qb, ub, vb):
        for n in range(NX):
            xx = lax.rem(x + 1 + n, NX)
            val = block(xx * NC + c).astype(BF).astype(F32)
            rc(tb.at[n], qb.at[n], rs_s.at[i, n], rs_r.at[i, n], dp=mate).wait_recv()
            ub[n] = (val + qb[n].astype(F32)).astype(BF)
            if n < NX - 1:
                rc(ub.at[n], vb.at[n], rs_s.at[i, NX], rs_r.at[i, NX], dp=xx * NC + c).start()

    def rs_end(i, ub, vb):
        drain(vb, rs_r.at[i, NX])
        total = ub[NX - 1].astype(F32)
        for n in range(NX - 1):
            total = total + vb[n].astype(F32)
        return total

    def rs_sent(i, tb, vb):
        for n in range(NX):
            drain(tb.at[n], rs_s.at[i, n])
        drain(vb, rs_s.at[i, NX])

    def tkb(n):
        return tk.at[n]

    def pkb(h):
        return lambda n: pk.at[h, n]

    EH = eg.shape[-1]
    hidden = [None, None, None]

    def e_up(h):
        def step(n, carry):
            a = pk[h, n].reshape(RQ, F)
            return carry[0] + dot(a, egv[n]), carry[1] + dot(a, euv[n])
        zero = jnp.zeros((RQ, EH), F32)
        g, u = lax.fori_loop(0, ndp, step, (zero, zero))
        hidden[h] = silu_mul(g, u)

    def e_block(h):
        return lambda n: dot(hidden[h], edv[:, pl.ds(pl.multiple_of(n * F, F), F)])

    def e_start(h):
        e_up(h)
        rs_start(h, e_block(h), et.at[h], eq.at[h])

    def e_cross(h):
        rs_cross(h, e_block(h), et.at[h], eq.at[h], eun.at[h], ev.at[h])

    def e_end(h):
        w1[h] = (rs_end(h, eun.at[h], ev.at[h]) * col[h]).astype(BF).reshape(HZ, RZ, F)
        if h == 0:
            r1[OWN] = w1[0, OWN]
        send_slots(8 + h, h, -1, lambda zz, s: w1.at[h, s], lambda s: r1.at[s])

    def z_in(h):
        n = HZ - 1 if h == 0 else HZ
        drain(pk.at[h, d, pl.ds(0, n)], set_r.at[5 + h])
        dp_own(1 + h, pkb(h))

    def start():
        send_z(1, lambda zz: chz.at[zz], c1.at[z])
        vd = wt.at[2, mine, :]
        send_y(2, lambda yy: vd, vd)
        c1[z] = chz[z]
        ring_b(0)
        dp_own(0, tkb)

    def down_y():
        drain(wt.at[2, pl.ds(0, (NY - 1) * WR), :], set_r.at[2])

    def ids_z():
        drain(c1.at[pl.ds(0, NZ - 1)], set_r.at[1])
        send_y(3, lambda yy: c1, c2.at[y])
        c2[y] = c1[...]

    def ids_y():
        drain(c2.at[pl.ds(0, NY - 1)], set_r.at[3])
        ids = c2[...].reshape(nex, 128).astype(F32).astype(BF)
        rep = (div(iota((R, nex), 0), slots) == iota((R, nex), 1)).astype(BF)
        spread = dot(rep, ids)
        lane = y * slots + mod(iota((R, 128), 0), slots)
        pick = jnp.sum(jnp.where(iota((R, 128), 1) == lane, spread, 0.0), axis=1, keepdims=True)
        onehot[...] = (pick.astype(jnp.int32) == iota((R, T), 1)).astype(BF)
        pk0[...] = dot(onehot[...], tk[d]).astype(BF).reshape(NY, RY, F)
        send_y(4, lambda yy: pk0.at[yy], pk1.at[y])
        pk1[y] = pk0[y]

    def out_y():
        drain(pk1.at[pl.ds(0, NY - 1)], set_r.at[4])
        pk2[...] = dot(pm[...], pk1[...].reshape(R, F)).astype(BF).reshape(NZ, RZ, F)
        send_slots(5, 0, 1, lambda zz, s: pk2.at[zz], lambda s: pk.at[0, d, s])
        send_slots(6, 1, 1, lambda zz, s: pk2.at[zz], lambda s: pk.at[1, d, s - HZ])
        pk[0, d, OWN] = pk2[z]

    def gathered(h):
        dp_pass(1 + h, pkb(h))
        if h == 0:
            for load in loads[4:]:
                load.wait()
        dp_done(1 + h, pkb(h))

    def s_step(n, carry):
        a = tk[n]
        rows = pl.ds(pl.multiple_of(n * F, F), F)
        return carry[0] + dot(a, wt[0, rows, :]), carry[1] + dot(a, wt[1, rows, :])

    def s_block(n):
        return dot_nt(hidden[2], wt[2, pl.ds(pl.multiple_of(n * F, F), F), :])

    def s_up():
        dp_done(0, tkb)
        drain(wt.at[pl.ds(0, 2), pl.ds(0, NZ * WR), :], set_r.at[0])
        zero = jnp.zeros((T, sg.shape[1]), F32)
        g, u = lax.fori_loop(0, ndp, s_step, (zero, zero))
        hidden[2] = silu_mul(g, u)

    def back_z():
        drain(r1.at[pl.ds(0, HZ - 1)], set_r.at[8])
        drain(r1.at[pl.ds(0, HZ)], set_r.at[9])
        w2[...] = dot(um[...], r1[...].reshape(R, F)).astype(BF).reshape(NY, RY, F)
        send_y(7, lambda yy: w2.at[yy], r2.at[y])
        r2[y] = w2[y]

    def s_end():
        shared_sum[...] = rs_end(3, sun, sv)

    def back_y():
        drain(r2.at[pl.ds(0, NY - 1)], set_r.at[7])
        out[...] = (shared_sum[...] + dot_tn(onehot[...], r2[...].reshape(R, F))).astype(BF)

    steps = {
        "start": start, "dy": down_y, "iz": ids_z, "iy": ids_y, "oy": out_y, "tk": lambda: dp_pass(0, tkb),
        "z0": lambda: z_in(0), "z1": lambda: z_in(1), "g0": lambda: gathered(0), "g1": lambda: gathered(1),
        "e0": lambda: e_start(0), "e1": lambda: e_start(1), "x0": lambda: e_cross(0), "x1": lambda: e_cross(1),
        "w0": lambda: e_end(0), "w1": lambda: e_end(1), "su": s_up, "ss": lambda: rs_start(3, s_block, st, sq),
        "sx": lambda: rs_cross(3, s_block, st, sq, sun, sv), "bz": back_z, "se": s_end, "by": back_y,
    }
    for k in range(1, CW + 2):
        steps[f"r{k}"] = functools.partial(ring, k)
    for name in ORDER(CW + 1):
        steps[name]()

    drain(wt.at[pl.ds(0, 2), pl.ds(0, NZ * (NY - 1) * WR), :], set_s.at[0])
    drain(c1.at[pl.ds(0, NZ - 1)], set_s.at[1])
    drain(wt.at[2, pl.ds(0, (NY - 1) * WR), :], set_s.at[2])
    drain(c2.at[pl.ds(0, NY - 1)], set_s.at[3])
    drain(pk1.at[pl.ds(0, NY - 1)], set_s.at[4])
    drain(pk2.at[pl.ds(0, HZ - 1)], set_s.at[5])
    drain(pk2.at[pl.ds(0, HZ)], set_s.at[6])
    drain(r2.at[pl.ds(0, NY - 1)], set_s.at[7])
    drain(r1.at[pl.ds(0, HZ - 1)], set_s.at[8])
    drain(r1.at[pl.ds(0, HZ)], set_s.at[9])
    dp_sent(0, tkb)
    for h in range(2):
        dp_sent(1 + h, pkb(h))
        rs_sent(h, et.at[h], ev.at[h])
    rs_sent(3, st, sv)
    for side, n in ((0, CW), (1, CCW)):
        for k in range(n):
            bsend(k, side).wait_send()
            for h in range(AH):
                asend(k, side, h).wait_send()


def shards(ndp, nex, tokens, chosen, counts, gates, eg, eu, ed, sg, su, sd):
    NX, NZ = ndp // NC, nex // NY
    slots = chosen.shape[2]
    T, F = tokens.shape
    D = F * ndp
    R = nex * slots
    RZ, RY = NY * slots, NZ * slots
    HZ, RQ = NZ // 2, R // 2
    WR, SHD = sg.shape
    EHD = eg.shape[-1]
    CW = NZ // 2
    vm = pl.BlockSpec(memory_space=pltpu.VMEM)
    hbm = pl.BlockSpec(memory_space=pltpu.HBM)
    return pl.pallas_call(
        functools.partial(kernel, ndp, nex, slots),
        out_shape=jax.ShapeDtypeStruct((T, F), BF),
        in_specs=[hbm, vm, vm, vm] + [hbm] * 6,
        out_specs=vm,
        scratch_shapes=[
            pltpu.VMEM((3, D, SHD), BF),
            pltpu.VMEM((ndp, T, F), BF),
            pltpu.VMEM((2, ndp, HZ, RZ, F), BF),
            pltpu.VMEM((ndp, F, EHD), BF),
            pltpu.VMEM((ndp, F, EHD), BF),
            pltpu.VMEM((EHD, D), BF),
            pltpu.VMEM((NZ, 1, 128), jnp.int32),
            pltpu.VMEM((NZ, 1, 128), jnp.int32),
            pltpu.VMEM((NY, NZ, 1, 128), jnp.int32),
            pltpu.VMEM((R, T), BF),
            pltpu.VMEM((R, R), BF),
            pltpu.VMEM((R, R), BF),
            pltpu.VMEM((2, RQ, 1), F32),
            pltpu.VMEM((NY, RY, F), BF),
            pltpu.VMEM((NY, RY, F), BF),
            pltpu.VMEM((NZ, RZ, F), BF),
            pltpu.VMEM((2, HZ, RZ, F), BF),
            pltpu.VMEM((NZ, RZ, F), BF),
            pltpu.VMEM((NY, RY, F), BF),
            pltpu.VMEM((NY, RY, F), BF),
            pltpu.VMEM((T, F), F32),
            pltpu.VMEM((2, NX, RQ, F), BF),
            pltpu.VMEM((2, NX, RQ, F), BF),
            pltpu.VMEM((2, NX, RQ, F), BF),
            pltpu.VMEM((2, NX - 1, RQ, F), BF),
            pltpu.VMEM((NX, T, F), BF),
            pltpu.VMEM((NX, T, F), BF),
            pltpu.VMEM((NX, T, F), BF),
            pltpu.VMEM((NX - 1, T, F), BF),
            pltpu.SemaphoreType.DMA((7,)),
            pltpu.SemaphoreType.DMA((2, NZ)),
            pltpu.SemaphoreType.DMA((1 + AH, 2, CW)),
            pltpu.SemaphoreType.DMA((1 + AH, 2, CW)),
            pltpu.SemaphoreType.DMA((10,)),
            pltpu.SemaphoreType.DMA((10,)),
            pltpu.SemaphoreType.DMA((3, NX)),
            pltpu.SemaphoreType.DMA((3, NX)),
            pltpu.SemaphoreType.DMA((4, NX + 1)),
            pltpu.SemaphoreType.DMA((4, NX + 1)),
        ],
        compiler_params=pltpu.CompilerParams(
            collective_id=0, has_side_effects=True, vmem_limit_bytes=60 * 1024 * 1024
        ),
    )(
        tokens, chosen[0].T, gates[0].T, counts,
        eg.reshape(ndp, F, EHD), eu.reshape(ndp, F, EHD), ed[0], sg, su, sd.T,
    )


def solution(mesh):
    return jax.shard_map(
        functools.partial(shards, mesh.shape["dp"], mesh.shape["expert"]),
        mesh=mesh,
        in_specs=(
            P("expert", "dp"),
            P("expert", None, None),
            P("expert", None),
            P("expert", None, None),
            P("expert", None, "dp"),
            P("expert", None, "dp"),
            P("expert", "dp", None),
            P("expert", "dp"),
            P("expert", "dp"),
            P("dp", "expert"),
        ),
        out_specs=P("expert", "dp"),
        check_vma=False,
    )
```

```python
import functools

import jax
import jax.numpy as jnp
from jax import lax
from jax.experimental import pallas as pl
from jax.experimental.pallas import tpu as pltpu
from jax.sharding import PartitionSpec as P

NC = 2
NY = 4

STEPS = (
    ("start", "dy", "r1", "iz", "r2", "iy", "r3", "oy", "r4", "tk", "z0", "r5", "z1", "r6"),
    ("g0", "e0", "x0", "r7", "g1", "e1", "x1", "r8", "r9", "w0"),
    ("su", "w1", "ss", "sx", "bz", "se", "by"),
)


def ORDER(last):
    names = [name for part in STEPS for name in part]
    return [n for n in names if not (n[0] == "r" and int(n[1:]) > last)]


AH = 1
BF = jnp.bfloat16
F32 = jnp.float32
MESH = pl.DeviceIdType.MESH


def iota(shape, dim):
    return lax.broadcasted_iota(jnp.int32, shape, dim)


def div(v, n):
    return v >> (n.bit_length() - 1)


def mod(v, n):
    return v & (n - 1)


def dot(a, b):
    return jnp.dot(a, b, preferred_element_type=F32)


def dot_nt(a, b):
    return lax.dot_general(a, b, (((1,), (1,)), ((), ())), preferred_element_type=F32)


def dot_tn(a, b):
    return lax.dot_general(a, b, (((0,), (0,)), ((), ())), preferred_element_type=F32)


def silu_mul(g, u):
    return (g / (1.0 + jnp.exp(-g)) * u).astype(BF)


def kernel(
    ndp, nex, slots,
    tok, ch, gates, counts, eg, eu, ed, sg, su, sd,
    out,
    wt, tk, pk, egv, euv, edv, chz, c1, c2, onehot, pm, um, col,
    pk0, pk1, pk2, w1, r1, w2, r2, shared_sum,
    et, eq, eun, ev, st, sq, sun, sv,
    loc, sp_r, ring_s, ring_r, set_s, set_r, x_s, x_r, rs_s, rs_r,
):
    NX = ndp // NC
    NZ = nex // NY
    T, F = tok.shape
    R = nex * slots
    RZ = NY * slots
    RY = NZ * slots
    HZ = NZ // 2
    RQ = R // 2
    OWN = NZ // 4 - 1
    d = lax.axis_index("dp")
    e = lax.axis_index("expert")
    x, c = div(d, NC), mod(d, NC)
    z, y = div(e, NY), mod(e, NY)
    mate = x * NC + (1 - c)
    WR = sg.shape[0]

    def zmod(v):
        return lax.rem(v + 2 * NZ, NZ)

    def at_z(k):
        return zmod(z + k) * NY + y

    def at_y(k):
        return z * NY + lax.rem(y + k, NY)

    def at_x(k):
        return lax.rem(x + k, NX) * NC + c

    def rc(src, dst, ss, rs, dp=None, ex=None):
        return pltpu.make_async_remote_copy(
            src_ref=src, dst_ref=dst, send_sem=ss, recv_sem=rs,
            device_id=(d if dp is None else dp, e if ex is None else ex), device_id_type=MESH,
        )

    def drain(view, sem):
        pltpu.make_async_copy(view, view, sem).wait()

    bar = pltpu.get_barrier_semaphore()

    def greet(dp, ex):
        pl.semaphore_signal(bar, inc=1, device_id=(dp, ex), device_id_type=MESH)

    def greet_z(k, carry):
        greet(d, at_z(k))
        return carry

    lax.fori_loop(1, NZ, greet_z, 0)
    for k in range(1, NY):
        greet(d, at_y(k))
    for k in range(1, NX):
        greet(at_x(k), e)
    greet(mate, e)

    def wrow1(zc, yc):
        return pl.ds(pl.multiple_of((zc * NY + yc) * WR, WR), WR)

    mine = wrow1(z, y)
    loads = [
        pltpu.make_async_copy(src, dst, loc.at[i])
        for i, (src, dst) in enumerate([
            (sg, wt.at[0, mine, :]), (su, wt.at[1, mine, :]), (sd, wt.at[2, mine, :]), (tok, tk.at[d]),
            (eg, egv), (eu, euv), (ed, edv),
        ])
    ]
    for load in loads:
        load.start()

    ids = jnp.zeros((NZ, 128), F32)
    for s in range(slots):
        row = ch[pl.ds(s, 1), :].astype(F32)
        own = jnp.where(div(iota((NZ, nex), 1), NY) == iota((NZ, nex), 0), row, 0.0).astype(BF)
        place = iota((nex, 128), 1) == mod(iota((nex, 128), 0), NY) * slots + s
        ids = ids + dot(own, place.astype(BF))
    chz[...] = ids.astype(jnp.int32).reshape(NZ, 1, 128)

    r, q = iota((R, R), 0), iota((R, R), 1)
    pm[...] = (mod(div(r, slots), NY) * RY + div(r, RZ) * slots + mod(r, slots) == q).astype(BF)
    zoff = mod(div(r, slots) - z + OWN + NZ, NZ)
    um[...] = (zoff * RZ + div(r, RY) * slots + mod(r, slots) == q).astype(BF)

    live = iota(gates.shape, 0) < counts[...]
    weight = jnp.where(live, gates[...], 0.0)
    for h in range(2):
        r, lane = iota((RQ, nex), 0), iota((RQ, nex), 1)
        owner = mod(z - (h * HZ - OWN) - div(r, RZ) + 2 * NZ, NZ) * NY + mod(div(r, slots), NY)
        picked = jnp.zeros((RQ, nex), F32)
        for s in range(slots):
            picked = jnp.where((lane == owner) & (mod(r, slots) == s), weight[s:s + 1, :], picked)
        col[h] = jnp.sum(picked, axis=1, keepdims=True)

    for load in loads[:4]:
        load.wait()
    pl.semaphore_wait(bar, (NZ - 1) + (NY - 1) + (NX - 1) + 1)

    def send_z(i, src, dst):
        def one(k, carry):
            zz = zmod(z + k)
            rc(src(zz), dst, set_s.at[i], set_r.at[i], ex=zz * NY + y).start()
            return carry
        lax.fori_loop(1, NZ, one, 0)

    def send_slots(i, h, sign, src, dst):
        def one(s, carry):
            zz = zmod(z + sign * (s - OWN))
            rc(src(zz, s - h * HZ), dst(s), set_s.at[i], set_r.at[i], ex=zz * NY + y).start()
            return carry
        if h == 0:
            lax.fori_loop(0, OWN, one, 0)
            lax.fori_loop(OWN + 1, HZ, one, 0)
        else:
            lax.fori_loop(HZ, NZ, one, 0)

    def send_y(i, src, dst):
        for k in range(1, NY):
            yy = lax.rem(y + k, NY)
            rc(src(yy), dst, set_s.at[i], set_r.at[i], ex=z * NY + yy).start()

    CW = NZ // 2
    CCW = NZ - 1 - CW

    def bsend(k, side):
        rows = wrow1(zmod(z - k) if side == 0 else zmod(z + k), y)
        v = wt.at[pl.ds(0, 2), rows, :]
        return rc(v, v, ring_s.at[0, side, k], ring_r.at[0, side, k], ex=at_z(1 if side == 0 else -1))

    def asend(k, side, h):
        zc = zmod(z - k) if side == 0 else zmod(z + k)
        n = NY * WR // AH
        v = wt.at[2, pl.ds(pl.multiple_of(zc * (NY * WR) + h * n, n), n), :]
        return rc(v, v, ring_s.at[1 + h, side, k], ring_r.at[1 + h, side, k], ex=at_z(1 if side == 0 else -1))

    def spread_to(j, zc, yc, side):
        v = wt.at[pl.ds(0, 2), wrow1(zc, yc), :]
        return rc(v, v, set_s.at[0], sp_r.at[side, j], ex=at_y(1 if side == 0 else NY - 1))

    def bspread(j, zc):
        spread_to(j, zc, y, 0).start()
        spread_to(j, zc, y, 1).start()

    def bpass(j, zc):
        for side in range(2):
            yc = lax.rem(y + (NY - 1 if side == 0 else 1), NY)
            spread_to(j, zc, yc, side).wait_recv()
            v = wt.at[side, wrow1(zc, yc), :]
            rc(v, v, set_s.at[0], set_r.at[0], ex=at_y(1 if side == 0 else NY - 1)).start()

    def bround(k, do):
        if k == 0:
            do(0, z)
        if 1 <= k <= CW:
            do(2 * k - 1, zmod(z - k))
        if 1 <= k <= CCW:
            do(2 * k, zmod(z + k))

    def ring_b(k):
        if k == 0:
            bsend(0, 0).start()
            bsend(0, 1).start()
            bround(0, bspread)
            return
        if k <= CW:
            bsend(k - 1, 0).wait_recv()
            if k < CW:
                bsend(k, 0).start()
        if k <= CCW:
            bsend(k - 1, 1).wait_recv()
            if k < CCW:
                bsend(k, 1).start()
        bround(k, bspread)

    def ring_a(k):
        for h in range(AH):
            if k == 0:
                asend(0, 0, h).start()
                asend(0, 1, h).start()
                continue
            if k <= CW:
                asend(k - 1, 0, h).wait_recv()
                if k < CW:
                    asend(k, 0, h).start()
            if k <= CCW:
                asend(k - 1, 1, h).wait_recv()
                if k < CCW:
                    asend(k, 1, h).start()

    def ring(k):
        if k <= CW:
            ring_b(k)
        bround(k - 1, bpass)
        if 1 <= k <= CW + 1:
            ring_a(k - 1)

    XORDER = sorted(range(1, NX), key=lambda k: min(k, NX - k))

    def dp_own(i, buf):
        for k in range(1, NX):
            rc(buf(d), buf(d), x_s.at[i, k], x_r.at[i, k], dp=at_x(k)).start()
        rc(buf(d), buf(d), x_s.at[i, 0], x_r.at[i, 0], dp=mate).start()

    def dp_pass(i, buf):
        for k in XORDER:
            src = buf(at_x(NX - k))
            rc(src, src, x_s.at[i, k], x_r.at[i, k], dp=at_x(k)).wait_recv()
            rc(src, src, x_s.at[i, 0], x_r.at[i, 0], dp=mate).start()

    def dp_done(i, buf):
        drain(buf(pl.ds(0, NX)), x_r.at[i, 0])

    def dp_sent(i, buf):
        drain(buf(pl.ds(0, NX)), x_s.at[i, 0])
        for k in range(1, NX):
            drain(buf(0), x_s.at[i, k])

    def rs_start(i, block, tb, qb):
        for n in range(NX):
            xx = lax.rem(x + 1 + n, NX)
            tb[n] = block(xx * NC + (1 - c)).astype(BF)
            rc(tb.at[n], qb.at[n], rs_s.at[i, n], rs_r.at[i, n], dp=mate).start()

    def rs_cross(i, block, tb, qb, ub, vb):
        for n in range(NX):
            xx = lax.rem(x + 1 + n, NX)
            val = block(xx * NC + c).astype(BF).astype(F32)
            rc(tb.at[n], qb.at[n], rs_s.at[i, n], rs_r.at[i, n], dp=mate).wait_recv()
            ub[n] = (val + qb[n].astype(F32)).astype(BF)
            if n < NX - 1:
                rc(ub.at[n], vb.at[n], rs_s.at[i, NX], rs_r.at[i, NX], dp=xx * NC + c).start()

    def rs_end(i, ub, vb):
        drain(vb, rs_r.at[i, NX])
        total = ub[NX - 1].astype(F32)
        for n in range(NX - 1):
            total = total + vb[n].astype(F32)
        return total

    def rs_sent(i, tb, vb):
        for n in range(NX):
            drain(tb.at[n], rs_s.at[i, n])
        drain(vb, rs_s.at[i, NX])

    def tkb(n):
        return tk.at[n]

    def pkb(h):
        return lambda n: pk.at[h, n]

    EH = eg.shape[-1]
    hidden = [None, None, None]

    def e_up(h):
        def step(n, carry):
            a = pk[h, n].reshape(RQ, F)
            return carry[0] + dot(a, egv[n]), carry[1] + dot(a, euv[n])
        zero = jnp.zeros((RQ, EH), F32)
        g, u = lax.fori_loop(0, ndp, step, (zero, zero))
        hidden[h] = silu_mul(g, u)

    def e_block(h):
        return lambda n: dot(hidden[h], edv[:, pl.ds(pl.multiple_of(n * F, F), F)])

    def e_start(h):
        e_up(h)
        rs_start(h, e_block(h), et.at[h], eq.at[h])

    def e_cross(h):
        rs_cross(h, e_block(h), et.at[h], eq.at[h], eun.at[h], ev.at[h])

    def e_end(h):
        w1[h] = (rs_end(h, eun.at[h], ev.at[h]) * col[h]).astype(BF).reshape(HZ, RZ, F)
        if h == 0:
            r1[OWN] = w1[0, OWN]
        send_slots(8 + h, h, -1, lambda zz, s: w1.at[h, s], lambda s: r1.at[s])

    def z_in(h):
        n = HZ - 1 if h == 0 else HZ
        drain(pk.at[h, d, pl.ds(0, n)], set_r.at[5 + h])
        dp_own(1 + h, pkb(h))

    def start():
        send_z(1, lambda zz: chz.at[zz], c1.at[z])
        vd = wt.at[2, mine, :]
        send_y(2, lambda yy: vd, vd)
        c1[z] = chz[z]
        ring_b(0)
        dp_own(0, tkb)

    def down_y():
        drain(wt.at[2, pl.ds(0, (NY - 1) * WR), :], set_r.at[2])

    def ids_z():
        drain(c1.at[pl.ds(0, NZ - 1)], set_r.at[1])
        send_y(3, lambda yy: c1, c2.at[y])
        c2[y] = c1[...]

    def ids_y():
        drain(c2.at[pl.ds(0, NY - 1)], set_r.at[3])
        ids = c2[...].reshape(nex, 128).astype(F32).astype(BF)
        rep = (div(iota((R, nex), 0), slots) == iota((R, nex), 1)).astype(BF)
        spread = dot(rep, ids)
        lane = y * slots + mod(iota((R, 128), 0), slots)
        pick = jnp.sum(jnp.where(iota((R, 128), 1) == lane, spread, 0.0), axis=1, keepdims=True)
        onehot[...] = (pick.astype(jnp.int32) == iota((R, T), 1)).astype(BF)
        pk0[...] = dot(onehot[...], tk[d]).astype(BF).reshape(NY, RY, F)
        send_y(4, lambda yy: pk0.at[yy], pk1.at[y])
        pk1[y] = pk0[y]

    def out_y():
        drain(pk1.at[pl.ds(0, NY - 1)], set_r.at[4])
        pk2[...] = dot(pm[...], pk1[...].reshape(R, F)).astype(BF).reshape(NZ, RZ, F)
        send_slots(5, 0, 1, lambda zz, s: pk2.at[zz], lambda s: pk.at[0, d, s])
        send_slots(6, 1, 1, lambda zz, s: pk2.at[zz], lambda s: pk.at[1, d, s - HZ])
        pk[0, d, OWN] = pk2[z]

    def gathered(h):
        dp_pass(1 + h, pkb(h))
        if h == 0:
            for load in loads[4:]:
                load.wait()
        dp_done(1 + h, pkb(h))

    def s_step(n, carry):
        a = tk[n]
        rows = pl.ds(pl.multiple_of(n * F, F), F)
        return carry[0] + dot(a, wt[0, rows, :]), carry[1] + dot(a, wt[1, rows, :])

    def s_block(n):
        return dot_nt(hidden[2], wt[2, pl.ds(pl.multiple_of(n * F, F), F), :])

    def s_up():
        dp_done(0, tkb)
        drain(wt.at[pl.ds(0, 2), pl.ds(0, NZ * WR), :], set_r.at[0])
        zero = jnp.zeros((T, sg.shape[1]), F32)
        g, u = lax.fori_loop(0, ndp, s_step, (zero, zero))
        hidden[2] = silu_mul(g, u)

    def back_z():
        drain(r1.at[pl.ds(0, HZ - 1)], set_r.at[8])
        drain(r1.at[pl.ds(0, HZ)], set_r.at[9])
        w2[...] = dot(um[...], r1[...].reshape(R, F)).astype(BF).reshape(NY, RY, F)
        send_y(7, lambda yy: w2.at[yy], r2.at[y])
        r2[y] = w2[y]

    def s_end():
        shared_sum[...] = rs_end(3, sun, sv)

    def back_y():
        drain(r2.at[pl.ds(0, NY - 1)], set_r.at[7])
        out[...] = (shared_sum[...] + dot_tn(onehot[...], r2[...].reshape(R, F))).astype(BF)

    steps = {
        "start": start, "dy": down_y, "iz": ids_z, "iy": ids_y, "oy": out_y, "tk": lambda: dp_pass(0, tkb),
        "z0": lambda: z_in(0), "z1": lambda: z_in(1), "g0": lambda: gathered(0), "g1": lambda: gathered(1),
        "e0": lambda: e_start(0), "e1": lambda: e_start(1), "x0": lambda: e_cross(0), "x1": lambda: e_cross(1),
        "w0": lambda: e_end(0), "w1": lambda: e_end(1), "su": s_up, "ss": lambda: rs_start(3, s_block, st, sq),
        "sx": lambda: rs_cross(3, s_block, st, sq, sun, sv), "bz": back_z, "se": s_end, "by": back_y,
    }
    for k in range(1, CW + 2):
        steps[f"r{k}"] = functools.partial(ring, k)
    for name in ORDER(CW + 1):
        steps[name]()

    drain(wt.at[pl.ds(0, 2), pl.ds(0, NZ * (NY - 1) * WR), :], set_s.at[0])
    drain(c1.at[pl.ds(0, NZ - 1)], set_s.at[1])
    drain(wt.at[2, pl.ds(0, (NY - 1) * WR), :], set_s.at[2])
    drain(c2.at[pl.ds(0, NY - 1)], set_s.at[3])
    drain(pk1.at[pl.ds(0, NY - 1)], set_s.at[4])
    drain(pk2.at[pl.ds(0, HZ - 1)], set_s.at[5])
    drain(pk2.at[pl.ds(0, HZ)], set_s.at[6])
    drain(r2.at[pl.ds(0, NY - 1)], set_s.at[7])
    drain(r1.at[pl.ds(0, HZ - 1)], set_s.at[8])
    drain(r1.at[pl.ds(0, HZ)], set_s.at[9])
    dp_sent(0, tkb)
    for h in range(2):
        dp_sent(1 + h, pkb(h))
        rs_sent(h, et.at[h], ev.at[h])
    rs_sent(3, st, sv)
    for side, n in ((0, CW), (1, CCW)):
        for k in range(n):
            bsend(k, side).wait_send()
            for h in range(AH):
                asend(k, side, h).wait_send()


def shards(ndp, nex, tokens, chosen, counts, gates, eg, eu, ed, sg, su, sd):
    NX, NZ = ndp // NC, nex // NY
    slots = chosen.shape[2]
    T, F = tokens.shape
    D = F * ndp
    R = nex * slots
    RZ, RY = NY * slots, NZ * slots
    HZ, RQ = NZ // 2, R // 2
    WR, SHD = sg.shape
    EHD = eg.shape[-1]
    CW = NZ // 2
    vm = pl.BlockSpec(memory_space=pltpu.VMEM)
    hbm = pl.BlockSpec(memory_space=pltpu.HBM)
    return pl.pallas_call(
        functools.partial(kernel, ndp, nex, slots),
        out_shape=jax.ShapeDtypeStruct((T, F), BF),
        in_specs=[hbm, vm, vm, vm] + [hbm] * 6,
        out_specs=vm,
        scratch_shapes=[
            pltpu.VMEM((3, D, SHD), BF),
            pltpu.VMEM((ndp, T, F), BF),
            pltpu.VMEM((2, ndp, HZ, RZ, F), BF),
            pltpu.VMEM((ndp, F, EHD), BF),
            pltpu.VMEM((ndp, F, EHD), BF),
            pltpu.VMEM((EHD, D), BF),
            pltpu.VMEM((NZ, 1, 128), jnp.int32),
            pltpu.VMEM((NZ, 1, 128), jnp.int32),
            pltpu.VMEM((NY, NZ, 1, 128), jnp.int32),
            pltpu.VMEM((R, T), BF),
            pltpu.VMEM((R, R), BF),
            pltpu.VMEM((R, R), BF),
            pltpu.VMEM((2, RQ, 1), F32),
            pltpu.VMEM((NY, RY, F), BF),
            pltpu.VMEM((NY, RY, F), BF),
            pltpu.VMEM((NZ, RZ, F), BF),
            pltpu.VMEM((2, HZ, RZ, F), BF),
            pltpu.VMEM((NZ, RZ, F), BF),
            pltpu.VMEM((NY, RY, F), BF),
            pltpu.VMEM((NY, RY, F), BF),
            pltpu.VMEM((T, F), F32),
            pltpu.VMEM((2, NX, RQ, F), BF),
            pltpu.VMEM((2, NX, RQ, F), BF),
            pltpu.VMEM((2, NX, RQ, F), BF),
            pltpu.VMEM((2, NX - 1, RQ, F), BF),
            pltpu.VMEM((NX, T, F), BF),
            pltpu.VMEM((NX, T, F), BF),
            pltpu.VMEM((NX, T, F), BF),
            pltpu.VMEM((NX - 1, T, F), BF),
            pltpu.SemaphoreType.DMA((7,)),
            pltpu.SemaphoreType.DMA((2, NZ)),
            pltpu.SemaphoreType.DMA((1 + AH, 2, CW)),
            pltpu.SemaphoreType.DMA((1 + AH, 2, CW)),
            pltpu.SemaphoreType.DMA((10,)),
            pltpu.SemaphoreType.DMA((10,)),
            pltpu.SemaphoreType.DMA((3, NX)),
            pltpu.SemaphoreType.DMA((3, NX)),
            pltpu.SemaphoreType.DMA((4, NX + 1)),
            pltpu.SemaphoreType.DMA((4, NX + 1)),
        ],
        compiler_params=pltpu.CompilerParams(
            collective_id=0, has_side_effects=True, vmem_limit_bytes=60 * 1024 * 1024
        ),
    )(
        tokens, chosen[0].T, gates[0].T, counts,
        eg.reshape(ndp, F, EHD), eu.reshape(ndp, F, EHD), ed[0], sg, su, sd.T,
    )


def solution(mesh):
    return jax.shard_map(
        functools.partial(shards, mesh.shape["dp"], mesh.shape["expert"]),
        mesh=mesh,
        in_specs=(
            P("expert", "dp"),
            P("expert", None, None),
            P("expert", None),
            P("expert", None, None),
            P("expert", None, "dp"),
            P("expert", None, "dp"),
            P("expert", "dp", None),
            P("expert", "dp"),
            P("expert", "dp"),
            P("dp", "expert"),
        ),
        out_specs=P("expert", "dp"),
        check_vma=False,
    )
```
